256 devices in a mesh: inner: 16 (over y, x), outer: 8 (over z_lo, core), head: 2 (over z_hi).
Axes of the slice: x: 4, y: 4, z: 8 (z_hi: 2, z_lo: 4; z = z_hi * 4 + z_lo), core: 2. Of those that a mesh axis runs over, the one named last changes fastest.
Arguments:
- query: bfloat16 [32768, 2048], P(('inner', 'outer'), 'head'), parts along dimension 1, may hold values from -4 to 4
- key: bfloat16 [32768, 256], P(('inner', 'outer'), 'head'), parts along dimension 1, may hold values from -4 to 4
- value: bfloat16 [32768, 256], P(('inner', 'outer'), 'head'), parts along dimension 1, may hold values from -6 to 6
- output: bfloat16 [32768, 2048], P(('inner', 'outer'), 'head'), parts along dimension 1, may hold values from -6 to 6
- grad_out: bfloat16 [32768, 2048], P(('inner', 'outer'), 'head'), parts along dimension 1, may hold values from -48 to 48
- lse: float32 [16, 32768], P('head', ('inner', 'outer')), parts along dimension 0
- block_order: int32 [1024], P('head'), parts along dimension 0, may hold values from 0 to 511, as said below
Outputs:
- grad_query: bfloat16 [32768, 2048], P(('inner', 'outer'), 'head'), parts along dimension 1
- grad_key: bfloat16 [32768, 256], P(('inner', 'outer'), 'head'), parts along dimension 1
- grad_value: bfloat16 [32768, 256], P(('inner', 'outer'), 'head'), parts along dimension 1
The draws below stay inside these ranges and needn't reach their ends.
There are 2 independent parts, one for each index of `head`. The reference program is written for one: setup_inputs(seed, part) draws one part's arguments, and reference() takes and returns one part's arrays. A program takes and returns all parts, laid end to end along the dimension named above; each array names one. Nothing has to cross between parts.
Inputs may be any that keep to these rules, and one draw needn't show every extreme that they name: `block_order`: a permutation of the 512 sequence blocks.
All inputs are finite; a program needn't handle non-finite values.
Results may differ from the reference program's by a relative error of at most 0.0051.
Values may be sent and summed in bfloat16 or wider, within the bound.
No kernel may reach another device: no remote copies, remote signals or barrier semaphores. Data moves between devices by JAX's collectives and lax.ppermute only.
A program may use at most 64 MiB of HBM per device.

```python
import jax
import jax.numpy as jnp
from jax import lax

H = 8
DH = 128
BLOCK = 64
TOK_DEV = 256
TOKENS = 32768
NBLK = 512
N_INNER = 16
N_OUTER = 8


def shuffled(base_key):
    return jax.random.permutation(jax.random.fold_in(base_key, 7), NBLK).astype(jnp.int32)


def draw_block_order(key, part):
    return shuffled(key)


def draw_lse(key, part):
    block_ids = shuffled(key)
    key = jax.random.fold_in(key, 5)
    row_ids = jnp.arange(TOKENS, dtype=jnp.int32)
    positions = (block_ids[row_ids // BLOCK] * BLOCK + row_ids % BLOCK).astype(jnp.float32)
    noise = jax.random.uniform(key, (H, TOKENS), jnp.float32, -0.5, 0.5)
    return jnp.log(2.0 * positions / N_OUTER + 1.0)[None, :] + 0.5 + noise


def draw_query(key, part):
    key = jax.random.fold_in(key, 11)
    values = jnp.clip(jax.random.normal(key, (TOKENS, H * DH), jnp.float32), -4.0, 4.0)
    return values.astype(jnp.bfloat16)


def draw_key(key, part):
    key = jax.random.fold_in(key, 13)
    values = jnp.clip(jax.random.normal(key, (TOKENS, DH), jnp.float32), -4.0, 4.0)
    return values.astype(jnp.bfloat16)


def block_scale(rng, dims, shards, least, largest):
    def one(axis_at, blocks):
        steps = jax.random.uniform(jax.random.fold_in(jax.random.fold_in(rng, 6), axis_at), (blocks,), jnp.float32, least / len(shards), largest / len(shards))
        return jnp.repeat(jnp.exp(steps), dims[axis_at] // blocks).reshape((-1,) + (1,) * (len(dims) - axis_at - 1))

    factor_of = one(*shards[0])
    for cut in shards[1:]:
        factor_of = factor_of * one(*cut)
    return factor_of


def scatter_about(own_key, extent, scale, most, cuts=(), kind=jnp.bfloat16):
    loudness = block_scale(own_key, extent, cuts, -0.22, 0.18) if cuts else 1.0
    result = jax.random.normal(own_key, extent, jnp.float32) * scale * loudness
    return jnp.minimum(jnp.maximum(result, -most), most).astype(kind)


def setup_inputs(seed: int = 0, part: int = 0) -> dict:
    key_of = jax.random.split(jax.random.key(seed), 8)
    part_splits = jax.random.split(jax.random.fold_in(key_of[7], part), 8)
    query = draw_query(jax.random.fold_in(jax.random.fold_in(key_of[7], part), 71), part)
    key = draw_key(jax.random.fold_in(jax.random.fold_in(key_of[7], part), 71), part)
    value = scatter_about(part_splits[2], (TOKENS, DH), 1.0, 6.0, ((0, 128),))
    output = scatter_about(part_splits[3], (TOKENS, H * DH), 1.0, 6.0, ((0, 128),))
    grad_out = scatter_about(part_splits[4], (TOKENS, H * DH), 8.0, 48.0, ((0, 128),))
    lse = draw_lse(jax.random.fold_in(jax.random.fold_in(key_of[7], part), 71), part)
    block_order = draw_block_order(jax.random.fold_in(jax.random.fold_in(key_of[7], part), 71), part)
    return {"query": query, "key": key, "value": value, "output": output, "grad_out": grad_out, "lse": lse, "block_order": block_order}


def reference(query, key, value, output, grad_out, lse, block_order):
    scaling = DH ** -0.5
    row_ids = jnp.arange(TOKENS, dtype=jnp.int32)
    positions = (block_order[row_ids // BLOCK] * BLOCK + row_ids % BLOCK).astype(jnp.int32)
    deltas = jnp.sum((grad_out.astype(jnp.float32) * output.astype(jnp.float32)).reshape(TOKENS, H, DH), axis=-1)

    def grouped(rows):
        return rows.reshape(N_INNER, N_OUTER, TOK_DEV, rows.shape[-1])

    q_grouped = grouped(query)
    out_grouped = grouped(grad_out)
    key_grouped = grouped(key)
    value_grouped = grouped(value)
    lse_grouped = grouped(lse.T)
    delta_grouped = grouped(deltas)
    pos_grouped = positions.reshape(N_INNER, N_OUTER, TOK_DEV)
    half = N_INNER * TOK_DEV

    def take_group(arr, group):
        return lax.dynamic_index_in_dim(arr, group, 1, keepdims=False)

    def per_group(totals, group):
        grad_keys, grad_values = totals
        prev = (group + N_OUTER - 1) % N_OUTER
        keys = jnp.concatenate([take_group(key_grouped, group).reshape(-1, DH), take_group(key_grouped, prev).reshape(-1, DH)], axis=0)
        values = jnp.concatenate([take_group(value_grouped, group).reshape(-1, DH), take_group(value_grouped, prev).reshape(-1, DH)], axis=0)
        key_pos = jnp.concatenate([take_group(pos_grouped, group).reshape(-1), take_group(pos_grouped, prev).reshape(-1)], axis=0)
        q_here = take_group(q_grouped, group)
        out_here = take_group(out_grouped, group)
        lse_here = take_group(lse_grouped, group)
        delta_here = take_group(delta_grouped, group)
        pos_here = take_group(pos_grouped, group)

        def per_shard(acc, shard):
            acc_keys, acc_values = acc
            q_rows = q_here[shard].reshape(TOK_DEV * H, DH)
            out_rows = out_here[shard].reshape(TOK_DEV * H, DH)
            lse_rows = lse_here[shard].reshape(-1)
            delta_rows = delta_here[shard].reshape(-1)
            query_positions = jnp.repeat(pos_here[shard], H)
            scores = jnp.dot(q_rows, keys.T, preferred_element_type=jnp.float32) * scaling
            visible = key_pos[None, :] <= query_positions[:, None]
            probs = jnp.where(visible, jnp.exp(scores - lse_rows[:, None]), jnp.zeros_like(scores))
            probs_low = probs.astype(jnp.bfloat16)
            acc_values = acc_values + jnp.dot(probs_low.T, out_rows, preferred_element_type=jnp.float32)
            grad_probs = jnp.dot(out_rows, values.T, preferred_element_type=jnp.float32)
            grad_scores = (probs * (grad_probs - delta_rows[:, None])).astype(jnp.bfloat16)
            grad_rows = jnp.dot(grad_scores, keys, preferred_element_type=jnp.float32) * scaling
            acc_keys = acc_keys + jnp.dot(grad_scores.T, q_rows, preferred_element_type=jnp.float32) * scaling
            return (acc_keys, acc_values), grad_rows.reshape(TOK_DEV, H * DH)

        zeros = jnp.zeros((2 * half, DH), jnp.float32)
        (acc_keys, acc_values), grad_rows = lax.scan(per_shard, (zeros, zeros), jnp.arange(N_INNER, dtype=jnp.int32))

        def place(total, acc):
            total = total.at[:, group].add(acc[:half].reshape(N_INNER, TOK_DEV, DH))
            return total.at[:, prev].add(acc[half:].reshape(N_INNER, TOK_DEV, DH))

        return (place(grad_keys, acc_keys), place(grad_values, acc_values)), grad_rows

    start_sums = (jnp.zeros((N_INNER, N_OUTER, TOK_DEV, DH), jnp.float32), jnp.zeros((N_INNER, N_OUTER, TOK_DEV, DH), jnp.float32))
    (grad_keys, grad_values), grad_blocks = lax.scan(per_group, start_sums, jnp.arange(N_OUTER, dtype=jnp.int32))
    grad_query = grad_blocks.transpose(1, 0, 2, 3).reshape(TOKENS, H * DH)
    return (grad_query.astype(jnp.bfloat16), grad_keys.reshape(TOKENS, DH).astype(jnp.bfloat16), grad_values.reshape(TOKENS, DH).astype(jnp.bfloat16))
```

```python
import functools
import math

import jax
import jax.numpy as jnp
from jax import lax
from jax.experimental import pallas as pl
from jax.experimental.pallas import tpu as pltpu
from jax.sharding import PartitionSpec as P

BLOCK = 64
SIDE = 4
UNIT = 256
BF16 = jnp.bfloat16
F32 = jnp.float32
STEPS = (0, 1, -1, 2)


def dot(a, b):
    return jnp.dot(a, b, preferred_element_type=F32)


def grads_kernel(*refs, parts, pieces, dq_in, dkv_in, dq_final, heads, head_dim):
    refs = list(refs)

    def take(n):
        out, refs[:] = refs[:n], refs[n:]
        return out

    rank_ref, nvis_ref, diag_ref = take(3)
    lse_ref, delta_ref = take(2)
    q_refs = take(parts)
    do_refs = take(parts)
    kv_refs = take(pieces)
    dq_in_refs = take(sum(dq_in))
    dkv_in_refs = take(pieces if dkv_in else 0)
    dq_refs = take(parts)
    dkv_refs = take(pieces)
    ks, vs, kt, qs, dos, qt, dot_t, dqt, dka, dva = take(10)

    scaling = head_dim**-0.5
    rate = scaling * math.log2(math.e)
    cols = heads * BLOCK
    per_part = q_refs[0].shape[0] // BLOCK
    per_piece = kv_refs[0].shape[0] // BLOCK
    blocks = per_piece * pieces

    for at, kv_ref in enumerate(kv_refs):

        @pl.loop(0, per_piece)
        def _(j, at=at, kv_ref=kv_ref):
            src = pl.multiple_of(j * BLOCK, BLOCK)
            dst = pl.multiple_of(rank_ref[at * per_piece + j] * BLOCK, BLOCK)
            ks[pl.ds(dst, BLOCK), :] = kv_ref[pl.ds(src, BLOCK), :head_dim]
            vs[pl.ds(dst, BLOCK), :] = kv_ref[pl.ds(src, BLOCK), head_dim:]
            if dkv_in:
                dka[pl.ds(dst, BLOCK), :] = dkv_in_refs[at][pl.ds(src, BLOCK), :head_dim]
                dva[pl.ds(dst, BLOCK), :] = dkv_in_refs[at][pl.ds(src, BLOCK), head_dim:]

    @pl.loop(0, blocks * BLOCK // UNIT)
    def _(j):
        kt[j] = ks[pl.ds(pl.multiple_of(j * UNIT, UNIT), UNIT), :].T

    if not dkv_in:
        dka[...] = jnp.zeros_like(dka)
        dva[...] = jnp.zeros_like(dva)

    for part in range(parts):
        for i in range(per_part):
            n = part * per_part + i
            for h in range(heads):
                rows = slice(i * BLOCK, (i + 1) * BLOCK)
                lanes = slice(h * head_dim, (h + 1) * head_dim)
                qs[n, h * BLOCK : (h + 1) * BLOCK, :] = q_refs[part][rows, lanes]
                dos[n, h * BLOCK : (h + 1) * BLOCK, :] = do_refs[part][rows, lanes]

    token = lax.broadcasted_iota(jnp.int32, (1, cols), 1) % BLOCK

    for part in range(parts):
        first = part * per_part
        given = dq_in_refs[sum(dq_in[:part])] if dq_in[part] else None

        @pl.loop(0, per_part)
        def _(i, first=first, given=given):
            n = first + i
            qt[...] = qs[n].T
            dot_t[...] = dos[n].T
            dqt[n] = jnp.zeros((head_dim, cols), F32) if given is None else given[i]
            visible = nvis_ref[n]
            units = (visible + (UNIT // BLOCK - 1)) // (UNIT // BLOCK)
            lse_row = lse_ref[pl.ds(n, 1), :]
            delta_row = delta_ref[pl.ds(n, 1), :]
            limit = jnp.where(diag_ref[n] > 0, token, BLOCK - 1) + (visible - 1) * BLOCK

            def tile(unit, count):
                for u in range(count):
                    start = pl.multiple_of((unit + u) * UNIT, UNIT)
                    here = pl.ds(start, UNIT)
                    scores = dot(ks[here, :], qt[...])
                    grad_probs = dot(vs[here, :], dot_t[...])
                    probs = jnp.exp2(scores * rate - lse_row)
                    row = lax.broadcasted_iota(jnp.int32, (UNIT, cols), 0)
                    probs = jnp.where(row <= limit - start, probs, 0.0)
                    grad_scores = (probs * (grad_probs - delta_row)).astype(BF16)
                    dva[here, :] += dot(probs.astype(BF16), dos[n])
                    dka[here, :] += dot(grad_scores, qs[n])
                    dqt[n] += dot(kt[unit + u], grad_scores)

            @pl.loop(0, units // 4)
            def _(t):
                tile(t * 4, 4)

            @pl.when(units % 4 >= 2)
            def _():
                tile(units // 4 * 4, 2)

            @pl.when(units % 2 == 1)
            def _():
                tile(units - 1, 1)

        for i in range(per_part):
            if dq_final[part]:
                rows_out = (dqt[first + i] * scaling).T.astype(dq_refs[part].dtype)
                for h in range(heads):
                    dq_refs[part][i * BLOCK : (i + 1) * BLOCK, h * head_dim : (h + 1) * head_dim] = rows_out[
                        h * BLOCK : (h + 1) * BLOCK, :
                    ]
            else:
                dq_refs[part][i] = dqt[first + i]

    for at, dkv_ref in enumerate(dkv_refs):

        @pl.loop(0, per_piece)
        def _(j, at=at, dkv_ref=dkv_ref):
            dst = pl.multiple_of(j * BLOCK, BLOCK)
            src = pl.multiple_of(rank_ref[at * per_piece + j] * BLOCK, BLOCK)
            factor = scaling if dkv_ref.dtype == BF16 else 1.0
            dkv_ref[pl.ds(dst, BLOCK), :head_dim] = (dka[pl.ds(src, BLOCK), :] * factor).astype(dkv_ref.dtype)
            dkv_ref[pl.ds(dst, BLOCK), head_dim:] = dva[pl.ds(src, BLOCK), :].astype(dkv_ref.dtype)


def grads(ranks, nvis, diag, lse, delta, qs, dos, kvs, dq_in, dkv_in, dq_out, dkv_dtypes):
    parts, pieces = len(qs), len(kvs)
    head_dim = kvs[0].shape[1] // 2
    heads = qs[0].shape[1] // head_dim
    cols = heads * BLOCK
    count = nvis.shape[0]
    rows = sum(kv.shape[0] for kv in kvs)
    per_part = qs[0].shape[0] // BLOCK
    smem, vmem = pl.BlockSpec(memory_space=pltpu.SMEM), pl.BlockSpec(memory_space=pltpu.VMEM)
    given = [d for d in dq_in if d is not None]
    args = [rank_arg for rank_arg in (ranks, nvis, diag)] + [lse, delta, *qs, *dos, *kvs, *given, *(dkv_in or [])]
    dq_shapes = [
        jax.ShapeDtypeStruct((per_part, head_dim, cols), F32) if d is None else jax.ShapeDtypeStruct(q.shape, d)
        for q, d in zip(qs, dq_out)
    ]
    dkv_shapes = [jax.ShapeDtypeStruct(kv.shape, d) for kv, d in zip(kvs, dkv_dtypes)]
    flops = 10 * count * cols * rows * head_dim // 2
    out = pl.pallas_call(
        functools.partial(
            grads_kernel,
            parts=parts,
            pieces=pieces,
            dq_in=tuple(int(d is not None) for d in dq_in),
            dkv_in=bool(dkv_in),
            dq_final=tuple(d is not None for d in dq_out),
            heads=heads,
            head_dim=head_dim,
        ),
        out_shape=tuple(dq_shapes + dkv_shapes),
        in_specs=[smem] * 3 + [vmem] * (len(args) - 3),
        out_specs=(vmem,) * (parts + pieces),
        scratch_shapes=[
            pltpu.VMEM((rows, head_dim), BF16),
            pltpu.VMEM((rows, head_dim), BF16),
            pltpu.VMEM((rows // UNIT, head_dim, UNIT), BF16),
            pltpu.VMEM((count, cols, head_dim), BF16),
            pltpu.VMEM((count, cols, head_dim), BF16),
            pltpu.VMEM((head_dim, cols), BF16),
            pltpu.VMEM((head_dim, cols), BF16),
            pltpu.VMEM((count, head_dim, cols), F32),
            pltpu.VMEM((rows, head_dim), F32),
            pltpu.VMEM((rows, head_dim), F32),
        ],
        compiler_params=pltpu.CompilerParams(vmem_limit_bytes=52 * 2**20),
        cost_estimate=pl.CostEstimate(flops=flops, bytes_accessed=2**23, transcendentals=count * cols * rows // 2),
    )(*args)
    return out[:parts], out[parts:]


def body(query, key, value, output, grad_out, lse, block_order):
    tokens_here = query.shape[0]
    per_device = tokens_here // BLOCK
    head_count = lse.shape[0]
    head_dim = key.shape[1]
    inner_count = lax.axis_size("inner")
    outer_count = lax.axis_size("outer")
    inner_index = lax.axis_index("inner")
    outer_index = lax.axis_index("outer")

    def moved(x, by, second):
        pairs = []
        for i in range(inner_count):
            y, x_at = divmod(i, SIDE)
            for o in range(outer_count):
                if (o % 2 == 0) != second:
                    to = y * SIDE + (x_at + by) % SIDE
                else:
                    to = (y + by) % SIDE * SIDE + x_at
                pairs.append((i * outer_count + o, to * outer_count + o))
        return lax.ppermute(x, ("inner", "outer"), pairs)

    def to_group(x, by):
        return lax.ppermute(x, "outer", [(i, (i + by) % outer_count) for i in range(outer_count)])

    def stat_rows(stats):
        return stats.reshape(head_count, per_device, BLOCK).transpose(1, 0, 2).reshape(per_device, -1)

    kv = jnp.concatenate([key, value], axis=1)
    row = [kv] + [moved(kv, by, False) for by in STEPS[1:]]
    own_row = jnp.concatenate(row, axis=0)
    rows = [own_row] + [moved(own_row, by, True) for by in STEPS[1:]]

    deltas = jnp.sum(
        (grad_out.astype(F32) * output.astype(F32)).reshape(tokens_here, head_count, head_dim), axis=-1
    ).T
    stats = jnp.stack([stat_rows(lse) * math.log2(math.e), stat_rows(deltas)])
    next_query = to_group(query, -1)
    next_grad_out = to_group(grad_out, -1)
    next_stats = to_group(stats, -1)

    ids = block_order.reshape(inner_count, outer_count, per_device)
    first = jnp.array(STEPS, jnp.int32)[None, :]
    second = jnp.array(STEPS, jnp.int32)[:, None]
    y, x = inner_index // SIDE, inner_index % SIDE
    even = outer_index % 2 == 0
    from_y = (y - jnp.where(even, second, first)) % SIDE
    from_x = (x - jnp.where(even, first, second)) % SIDE
    owner = (from_y * SIDE + from_x).reshape(-1)
    group_ids = lax.dynamic_index_in_dim(ids, outer_index, 1, keepdims=False)
    key_ids = jnp.take(group_ids, owner, axis=0).reshape(-1)
    own_ids = lax.dynamic_index_in_dim(group_ids, inner_index, 0, keepdims=False)
    next_ids = lax.dynamic_index_in_dim(
        lax.dynamic_index_in_dim(ids, (outer_index + 1) % outer_count, 1, keepdims=False),
        inner_index,
        0,
        keepdims=False,
    )
    query_ids = jnp.concatenate([own_ids, next_ids])

    def order(keys):
        return jnp.sum((keys[None, :] < keys[:, None]).astype(jnp.int32), axis=1)

    def seen(keys, queries):
        return (
            jnp.sum((keys[None, :] <= queries[:, None]).astype(jnp.int32), axis=1),
            jnp.sum((keys[None, :] == queries[:, None]).astype(jnp.int32), axis=1),
        )

    nvis, diag = seen(key_ids, query_ids)
    both = jnp.concatenate([stats, next_stats], axis=1)
    (dq_own, dq_next), dkv_rows = grads(
        order(key_ids),
        nvis,
        diag,
        both[0],
        both[1],
        [query, next_query],
        [grad_out, next_grad_out],
        rows,
        [None, None],
        None,
        [F32, BF16],
        [BF16] * 4,
    )
    dq_back = to_group(dq_next, 1)
    row_sum = dkv_rows[0].astype(F32)
    for by, part in zip(STEPS[1:], dkv_rows[1:]):
        row_sum = row_sum + moved(part, -by, True).astype(F32)
    row_low = row_sum.astype(BF16)
    total = row_sum[:tokens_here]
    for at, by in enumerate(STEPS[1:], 1):
        total = total + moved(row_low[at * tokens_here : (at + 1) * tokens_here], -by, False).astype(F32)
    return (
        (dq_own + dq_back.astype(F32)).astype(BF16),
        total[:, :head_dim].astype(BF16),
        total[:, head_dim:].astype(BF16),
    )


def solution(mesh):
    tokens = P(("inner", "outer"), "head")
    return jax.shard_map(
        body,
        mesh=mesh,
        in_specs=(tokens, tokens, tokens, tokens, tokens, P("head", ("inner", "outer")), P("head")),
        out_specs=(tokens, tokens, tokens),
        check_vma=False,
    )
```

```python
import functools
import math

import jax
import jax.numpy as jnp
from jax import lax
from jax.experimental import pallas as pl
from jax.experimental.pallas import tpu as pltpu
from jax.sharding import PartitionSpec as P

BLOCK = 64
SIDE = 4
UNIT = 256
GROUP = 4
BF16 = jnp.bfloat16
F32 = jnp.float32
STEPS = (0, 1, -1, 2)


def dot(a, b):
    return jnp.dot(a, b, preferred_element_type=F32)


def grads_kernel(*refs, parts, pieces, dq_in, dkv_in, dq_final, dkv_final, heads, head_dim):
    refs = list(refs)

    def take(n):
        out, refs[:] = refs[:n], refs[n:]
        return out

    rank_ref, nvis_ref, diag_ref = take(3)
    lse_ref, delta_ref = take(2)
    q_refs = take(parts)
    do_refs = take(parts)
    kv_refs = take(pieces)
    dq_in_refs = take(sum(dq_in))
    dkv_in_refs = take(pieces if dkv_in else 0)
    dq_refs = take(parts)
    dkv_refs = take(pieces)
    ks, vs, kt, qs, dos, qt, dot_t, dqt, dka, dva = take(10)

    scaling = head_dim**-0.5
    rate = scaling * math.log2(math.e)
    cols = heads * BLOCK
    per_part = q_refs[0].shape[0] // BLOCK
    per_piece = kv_refs[0].shape[0] // BLOCK
    blocks = per_piece * pieces

    for at, kv_ref in enumerate(kv_refs):

        @pl.loop(0, per_piece)
        def _(j, at=at, kv_ref=kv_ref):
            src = pl.multiple_of(j * BLOCK, BLOCK)
            dst = pl.multiple_of(rank_ref[at * per_piece + j] * BLOCK, BLOCK)
            ks[pl.ds(dst, BLOCK), :] = kv_ref[pl.ds(src, BLOCK), :head_dim]
            vs[pl.ds(dst, BLOCK), :] = kv_ref[pl.ds(src, BLOCK), head_dim:]
            if dkv_in:
                dka[pl.ds(dst, BLOCK), :] = dkv_in_refs[at][pl.ds(src, BLOCK), :head_dim]
                dva[pl.ds(dst, BLOCK), :] = dkv_in_refs[at][pl.ds(src, BLOCK), head_dim:]

    @pl.loop(0, blocks * BLOCK // UNIT)
    def _(j):
        kt[j] = ks[pl.ds(pl.multiple_of(j * UNIT, UNIT), UNIT), :].T

    if not dkv_in:
        dka[...] = jnp.zeros_like(dka)
        dva[...] = jnp.zeros_like(dva)

    token = lax.broadcasted_iota(jnp.int32, (1, cols), 1) % BLOCK

    for part in range(parts):
        first = part * per_part
        given = dq_in_refs[sum(dq_in[:part])] if dq_in[part] else None

        @pl.loop(0, per_part)
        def _(i, part=part, first=first, given=given):
            n = first + i
            rows_here = pl.ds(pl.multiple_of(i * BLOCK, BLOCK), BLOCK)
            for h in range(heads):
                lanes = slice(h * head_dim, (h + 1) * head_dim)
                qs[h * BLOCK : (h + 1) * BLOCK, :] = q_refs[part][rows_here, lanes]
                dos[h * BLOCK : (h + 1) * BLOCK, :] = do_refs[part][rows_here, lanes]
            qt[...] = qs[...].T
            dot_t[...] = dos[...].T
            dqt[...] = jnp.zeros((head_dim, cols), F32) if given is None else given[i]
            visible = nvis_ref[n]
            units = (visible + (UNIT // BLOCK - 1)) // (UNIT // BLOCK)
            lse_row = lse_ref[pl.ds(n, 1), :]
            delta_row = delta_ref[pl.ds(n, 1), :]
            limit = jnp.where(diag_ref[n] > 0, token, BLOCK - 1) + (visible - 1) * BLOCK

            def tile(unit, count, masked):
                for u in range(count):
                    start = pl.multiple_of((unit + u) * UNIT, UNIT)
                    here = pl.ds(start, UNIT)
                    scores = dot(ks[here, :], qt[...])
                    grad_probs = dot(vs[here, :], dot_t[...])
                    probs = jnp.exp2(scores * rate - lse_row)
                    if masked:
                        row = lax.broadcasted_iota(jnp.int32, (UNIT, cols), 0)
                        probs = jnp.where(row <= limit - start, probs, 0.0)
                    grad_scores = (probs * (grad_probs - delta_row)).astype(BF16)
                    dva[here, :] += dot(probs.astype(BF16), dos[...])
                    dka[here, :] += dot(grad_scores, qs[...])
                    dqt[...] += dot(kt[unit + u], grad_scores)

            clear = jnp.maximum(units - 1, 0) // GROUP
            rest = units - clear * GROUP

            @pl.loop(0, clear)
            def _(t):
                tile(t * GROUP, GROUP, False)

            for count in range(1, GROUP + 1):

                @pl.when(rest == count)
                def _(count=count):
                    tile(clear * GROUP, count, True)

            if dq_final[part]:
                rows_out = (dqt[...] * scaling).astype(dq_refs[part].dtype).T
                for h in range(heads):
                    dq_refs[part][rows_here, h * head_dim : (h + 1) * head_dim] = rows_out[
                        h * BLOCK : (h + 1) * BLOCK, :
                    ]
            else:
                dq_refs[part][i] = dqt[...]

    for at, dkv_ref in enumerate(dkv_refs):

        @pl.loop(0, per_piece)
        def _(j, at=at, dkv_ref=dkv_ref):
            dst = pl.multiple_of(j * BLOCK, BLOCK)
            src = pl.multiple_of(rank_ref[at * per_piece + j] * BLOCK, BLOCK)
            factor = scaling if dkv_final else 1.0
            dkv_ref[pl.ds(dst, BLOCK), :head_dim] = (dka[pl.ds(src, BLOCK), :] * factor).astype(dkv_ref.dtype)
            dkv_ref[pl.ds(dst, BLOCK), head_dim:] = dva[pl.ds(src, BLOCK), :].astype(dkv_ref.dtype)


def grads(ranks, nvis, diag, lse, delta, qs, dos, kvs, dq_in, dkv_in, dq_out, dkv_dtypes, dkv_final):
    parts, pieces = len(qs), len(kvs)
    head_dim = kvs[0].shape[1] // 2
    heads = qs[0].shape[1] // head_dim
    cols = heads * BLOCK
    count = nvis.shape[0]
    rows = sum(kv.shape[0] for kv in kvs)
    per_part = qs[0].shape[0] // BLOCK
    smem, vmem = pl.BlockSpec(memory_space=pltpu.SMEM), pl.BlockSpec(memory_space=pltpu.VMEM)
    given = [d for d in dq_in if d is not None]
    args = [ranks, nvis, diag, lse, delta, *qs, *dos, *kvs, *given, *(dkv_in or [])]
    dq_shapes = [
        jax.ShapeDtypeStruct((per_part, head_dim, cols), F32) if d is None else jax.ShapeDtypeStruct(q.shape, d)
        for q, d in zip(qs, dq_out)
    ]
    dkv_shapes = [jax.ShapeDtypeStruct(kv.shape, d) for kv, d in zip(kvs, dkv_dtypes)]
    flops = 10 * count * cols * rows * head_dim // 2
    out = pl.pallas_call(
        functools.partial(
            grads_kernel,
            parts=parts,
            pieces=pieces,
            dq_in=tuple(int(d is not None) for d in dq_in),
            dkv_in=bool(dkv_in),
            dq_final=tuple(d is not None for d in dq_out),
            dkv_final=dkv_final,
            heads=heads,
            head_dim=head_dim,
        ),
        out_shape=tuple(dq_shapes + dkv_shapes),
        in_specs=[smem] * 3 + [vmem] * (len(args) - 3),
        out_specs=(vmem,) * (parts + pieces),
        scratch_shapes=[
            pltpu.VMEM((rows, head_dim), BF16),
            pltpu.VMEM((rows, head_dim), BF16),
            pltpu.VMEM((rows // UNIT, head_dim, UNIT), BF16),
            pltpu.VMEM((cols, head_dim), BF16),
            pltpu.VMEM((cols, head_dim), BF16),
            pltpu.VMEM((head_dim, cols), BF16),
            pltpu.VMEM((head_dim, cols), BF16),
            pltpu.VMEM((head_dim, cols), F32),
            pltpu.VMEM((rows, head_dim), F32),
            pltpu.VMEM((rows, head_dim), F32),
        ],
        compiler_params=pltpu.CompilerParams(vmem_limit_bytes=28 * 2**20),
        cost_estimate=pl.CostEstimate(flops=flops, bytes_accessed=2**23, transcendentals=count * cols * rows // 2),
    )(*args)
    return out[:parts], out[parts:]


def body(query, key, value, output, grad_out, lse, block_order):
    tokens_here = query.shape[0]
    per_device = tokens_here // BLOCK
    head_count = lse.shape[0]
    head_dim = key.shape[1]
    inner_count = lax.axis_size("inner")
    outer_count = lax.axis_size("outer")
    inner_index = lax.axis_index("inner")
    outer_index = lax.axis_index("outer")

    def moved(x, by, second):
        pairs = []
        for i in range(inner_count):
            y, x_at = divmod(i, SIDE)
            for o in range(outer_count):
                if (o % 2 == 0) != second:
                    to = y * SIDE + (x_at + by) % SIDE
                else:
                    to = (y + by) % SIDE * SIDE + x_at
                pairs.append((i * outer_count + o, to * outer_count + o))
        return lax.ppermute(x, ("inner", "outer"), pairs)

    def to_group(x, by):
        return lax.ppermute(x, "outer", [(i, (i + by) % outer_count) for i in range(outer_count)])

    def stat_rows(stats):
        return stats.reshape(head_count, per_device, BLOCK).transpose(1, 0, 2).reshape(per_device, -1)

    zero = jnp.zeros((), BF16)
    kv = lax.pad(key, zero, ((0, 0, 0), (0, head_dim, 0))) + lax.pad(value, zero, ((0, 0, 0), (head_dim, 0, 0)))
    row = [kv] + [moved(kv, by, False) for by in STEPS[1:]]
    own_row = jnp.concatenate(row, axis=0)
    rows = [own_row] + [moved(own_row, by, True) for by in STEPS[1:]]

    deltas = jnp.sum(
        (grad_out.astype(F32) * output.astype(F32)).reshape(tokens_here, head_count, head_dim), axis=-1
    ).T
    stats = jnp.stack([stat_rows(lse) * math.log2(math.e), stat_rows(deltas)])
    next_query = to_group(query, -1)
    next_grad_out = to_group(grad_out, -1)
    next_stats = to_group(stats, -1)

    ids = block_order.reshape(inner_count, outer_count, per_device)
    first = jnp.array(STEPS, jnp.int32)[None, :]
    second = jnp.array(STEPS, jnp.int32)[:, None]
    y, x = inner_index // SIDE, inner_index % SIDE
    even = outer_index % 2 == 0
    from_y = (y - jnp.where(even, second, first)) % SIDE
    from_x = (x - jnp.where(even, first, second)) % SIDE
    owner = (from_y * SIDE + from_x).reshape(-1)
    group_ids = lax.dynamic_index_in_dim(ids, outer_index, 1, keepdims=False)
    key_ids = jnp.take(group_ids, owner, axis=0).reshape(-1)
    own_ids = lax.dynamic_index_in_dim(group_ids, inner_index, 0, keepdims=False)
    next_ids = lax.dynamic_index_in_dim(
        lax.dynamic_index_in_dim(ids, (outer_index + 1) % outer_count, 1, keepdims=False),
        inner_index,
        0,
        keepdims=False,
    )
    query_ids = jnp.concatenate([own_ids, next_ids])

    def order(keys):
        return jnp.sum((keys[None, :] < keys[:, None]).astype(jnp.int32), axis=1)

    def seen(keys, queries):
        return (
            jnp.sum((keys[None, :] <= queries[:, None]).astype(jnp.int32), axis=1),
            jnp.sum((keys[None, :] == queries[:, None]).astype(jnp.int32), axis=1),
        )

    both = jnp.concatenate([stats, next_stats], axis=1)
    row_ids, other_ids = jnp.split(key_ids, [own_row.shape[0] // BLOCK])
    row_rank = order(row_ids)
    (dq_own,), (dkv_row,) = grads(
        row_rank, *seen(row_ids, own_ids), stats[0], stats[1], [query], [grad_out], [own_row],
        [None], None, [None], [F32], False,
    )
    (dq_own, dq_next), dkv_rows = grads(
        order(other_ids), *seen(other_ids, query_ids), both[0], both[1],
        [query, next_query], [grad_out, next_grad_out], rows[1:],
        [dq_own, None], None, [F32, None], [BF16] * 3, True,
    )
    (dq_next,), (row_sum,) = grads(
        row_rank, *seen(row_ids, next_ids), next_stats[0], next_stats[1], [next_query], [next_grad_out], [own_row],
        [dq_next], [dkv_row], [BF16], [F32], True,
    )
    dq_back = to_group(dq_next, 1)
    for by, part in zip(STEPS[1:], dkv_rows):
        row_sum = row_sum + moved(part, -by, True).astype(F32)
    row_low = row_sum.astype(BF16)
    total = row_sum[:tokens_here]
    for at, by in enumerate(STEPS[1:], 1):
        total = total + moved(row_low[at * tokens_here : (at + 1) * tokens_here], -by, False).astype(F32)
    return (
        (dq_own + dq_back.astype(F32)).astype(BF16),
        total[:, :head_dim].astype(BF16),
        total[:, head_dim:].astype(BF16),
    )


def solution(mesh):
    tokens = P(("inner", "outer"), "head")
    return jax.shard_map(
        body,
        mesh=mesh,
        in_specs=(tokens, tokens, tokens, tokens, tokens, P("head", ("inner", "outer")), P("head")),
        out_specs=(tokens, tokens, tokens),
        check_vma=False,
    )
```

```python
import functools
import math

import jax
import jax.numpy as jnp
from jax import lax
from jax.experimental import pallas as pl
from jax.experimental.pallas import tpu as pltpu
from jax.sharding import PartitionSpec as P

BLOCK = 64
SIDE = 4
UNIT = 256
GROUP = 4
BF16 = jnp.bfloat16
F32 = jnp.float32
STEPS = (0, 1, -1, 2)
PIECES = 3


def dot(a, b):
    return jnp.dot(a, b, preferred_element_type=F32)


def grads_kernel(*refs, parts, pieces, dq_in, dkv_in, dq_final, dkv_final, heads, head_dim):
    refs = list(refs)

    def take(n):
        out, refs[:] = refs[:n], refs[n:]
        return out

    rank_ref, nvis_ref, diag_ref = take(3)
    packed_refs = take(parts)
    kv_refs = take(pieces)
    dq_in_refs = take(sum(dq_in))
    dkv_in_refs = take(pieces if dkv_in else 0)
    dq_refs = take(parts)
    dkv_refs = take(pieces)
    ks, vs, qs, dos, qt, dot_t, dqt, dka, dva, stat = take(10)

    scaling = head_dim**-0.5
    rate = scaling * math.log2(math.e)
    cols = heads * BLOCK
    tokens = (packed_refs[0].shape[0] - 2 * heads) // 2
    per_part = tokens // BLOCK
    per_piece = kv_refs[0].shape[0] // BLOCK

    for at, kv_ref in enumerate(kv_refs):

        @pl.loop(0, per_piece)
        def _(j, at=at, kv_ref=kv_ref):
            src = pl.multiple_of(j * BLOCK, BLOCK)
            dst = pl.multiple_of(rank_ref[at * per_piece + j] * BLOCK, BLOCK)
            ks[pl.ds(dst, BLOCK), :] = kv_ref[pl.ds(src, BLOCK), :head_dim]
            vs[pl.ds(dst, BLOCK), :] = kv_ref[pl.ds(src, BLOCK), head_dim:]
            if dkv_in:
                dka[pl.ds(dst, BLOCK), :] = dkv_in_refs[at][pl.ds(src, BLOCK), :head_dim]
                dva[pl.ds(dst, BLOCK), :] = dkv_in_refs[at][pl.ds(src, BLOCK), head_dim:]

    if not dkv_in:
        dka[...] = jnp.zeros_like(dka)
        dva[...] = jnp.zeros_like(dva)

    for part, packed in enumerate(packed_refs):
        pieces_of = [
            packed[2 * tokens :, piece * tokens : (piece + 1) * tokens].astype(F32) for piece in range(PIECES)
        ]
        whole = pieces_of[0] + pieces_of[1] + pieces_of[2]
        for i in range(per_part):
            n = part * per_part + i
            for h in range(heads):
                for kind in range(2):
                    stat[kind, n : n + 1, h * BLOCK : (h + 1) * BLOCK] = whole[
                        kind * heads + h : kind * heads + h + 1, i * BLOCK : (i + 1) * BLOCK
                    ]

    token = lax.broadcasted_iota(jnp.int32, (1, cols), 1) % BLOCK

    for part in range(parts):
        first = part * per_part
        given = dq_in_refs[sum(dq_in[:part])] if dq_in[part] else None

        @pl.loop(0, per_part)
        def _(i, part=part, first=first, given=given):
            n = first + i
            rows_here = pl.ds(pl.multiple_of(i * BLOCK, BLOCK), BLOCK)
            grad_rows_here = pl.ds(pl.multiple_of(tokens + i * BLOCK, BLOCK), BLOCK)
            for h in range(heads):
                lanes = slice(h * head_dim, (h + 1) * head_dim)
                qs[h * BLOCK : (h + 1) * BLOCK, :] = packed_refs[part][rows_here, lanes]
                dos[h * BLOCK : (h + 1) * BLOCK, :] = packed_refs[part][grad_rows_here, lanes]
            qt[...] = qs[...].T
            dot_t[...] = dos[...].T
            dqt[...] = jnp.zeros((head_dim, cols), F32) if given is None else given[i]
            visible = nvis_ref[n]
            units = (visible + (UNIT // BLOCK - 1)) // (UNIT // BLOCK)
            lse_row = stat[0, pl.ds(n, 1), :] * math.log2(math.e)
            delta_row = stat[1, pl.ds(n, 1), :]
            limit = jnp.where(diag_ref[n] > 0, token, BLOCK - 1) + (visible - 1) * BLOCK

            def tile(unit, count, masked):
                for u in range(count):
                    start = pl.multiple_of((unit + u) * UNIT, UNIT)
                    here = pl.ds(start, UNIT)
                    scores = dot(ks[here, :], qt[...])
                    grad_probs = dot(vs[here, :], dot_t[...])
                    probs = jnp.exp2(scores * rate - lse_row)
                    if masked:
                        row = lax.broadcasted_iota(jnp.int32, (UNIT, cols), 0)
                        probs = jnp.where(row <= limit - start, probs, 0.0)
                    grad_scores = (probs * (grad_probs - delta_row)).astype(BF16)
                    dva[here, :] += dot(probs.astype(BF16), dos[...])
                    dka[here, :] += dot(grad_scores, qs[...])
                    dqt[...] += lax.dot_general(
                        ks[here, :], grad_scores, (((0,), (0,)), ((), ())), preferred_element_type=F32
                    )

            clear = jnp.maximum(units - 1, 0) // GROUP
            rest = units - clear * GROUP

            @pl.loop(0, clear)
            def _(t):
                tile(t * GROUP, GROUP, False)

            for count in range(1, GROUP + 1):

                @pl.when(rest == count)
                def _(count=count):
                    tile(clear * GROUP, count, True)

            if dq_final[part]:
                rows_out = (dqt[...] * scaling).astype(dq_refs[part].dtype).T
                for h in range(heads):
                    dq_refs[part][rows_here, h * head_dim : (h + 1) * head_dim] = rows_out[
                        h * BLOCK : (h + 1) * BLOCK, :
                    ]
            else:
                dq_refs[part][i] = dqt[...]

    for at, dkv_ref in enumerate(dkv_refs):

        @pl.loop(0, per_piece)
        def _(j, at=at, dkv_ref=dkv_ref):
            dst = pl.multiple_of(j * BLOCK, BLOCK)
            src = pl.multiple_of(rank_ref[at * per_piece + j] * BLOCK, BLOCK)
            factor = scaling if dkv_final else 1.0
            dkv_ref[pl.ds(dst, BLOCK), :head_dim] = (dka[pl.ds(src, BLOCK), :] * factor).astype(dkv_ref.dtype)
            dkv_ref[pl.ds(dst, BLOCK), head_dim:] = dva[pl.ds(src, BLOCK), :].astype(dkv_ref.dtype)


def pack_kernel(q_ref, do_ref, out_ref, lse_ref, packed_ref, out_here, stat, sems, *, heads, head_dim):
    rows = q_ref.shape[0]
    copies = [
        pltpu.make_async_copy(do_ref, packed_ref.at[rows : 2 * rows, :], sems.at[0]),
        pltpu.make_async_copy(out_ref, out_here, sems.at[1]),
        pltpu.make_async_copy(lse_ref, stat.at[:heads, :], sems.at[2]),
        pltpu.make_async_copy(q_ref, packed_ref.at[:rows, :], sems.at[3]),
    ]
    for copy in copies:
        copy.start()
    for copy in copies[:3]:
        copy.wait()
    for h in range(heads):
        lanes = slice(h * head_dim, (h + 1) * head_dim)
        product = packed_ref[rows : 2 * rows, lanes].astype(F32) * out_here[:, lanes].astype(F32)
        stat[heads + h : heads + h + 1, :] = jnp.sum(product.T, axis=0, keepdims=True)
    left = stat[...]
    for piece in range(PIECES):
        low = left.astype(BF16)
        packed_ref[2 * rows :, piece * rows : (piece + 1) * rows] = low
        left = left - low.astype(F32)
    packed_ref[2 * rows :, PIECES * rows :] = jnp.zeros((2 * heads, packed_ref.shape[1] - PIECES * rows), BF16)
    copies[3].wait()


def pack(query, grad_out, output, lse):
    heads, rows = lse.shape
    return pl.pallas_call(
        functools.partial(pack_kernel, heads=heads, head_dim=query.shape[1] // heads),
        out_shape=jax.ShapeDtypeStruct((2 * rows + 2 * heads, query.shape[1]), BF16),
        in_specs=[pl.BlockSpec(memory_space=pltpu.HBM)] * 4,
        out_specs=pl.BlockSpec(memory_space=pltpu.VMEM),
        scratch_shapes=[
            pltpu.VMEM((rows, query.shape[1]), BF16),
            pltpu.VMEM((2 * heads, rows), F32),
            pltpu.SemaphoreType.DMA((4,)),
        ],
        compiler_params=pltpu.CompilerParams(vmem_limit_bytes=60 * 2**20),
        cost_estimate=pl.CostEstimate(flops=2 * query.size, bytes_accessed=2**22, transcendentals=0),
    )(query, grad_out, output, lse)


def grads(ranks, nvis, diag, packed, kvs, dq_in, dkv_in, dq_out, dkv_dtypes, dkv_final):
    parts, pieces = len(packed), len(kvs)
    head_dim = kvs[0].shape[1] // 2
    width = packed[0].shape[1]
    heads = width // head_dim
    cols = heads * BLOCK
    count = nvis.shape[0]
    rows = sum(kv.shape[0] for kv in kvs)
    tokens = (packed[0].shape[0] - 2 * heads) // 2
    per_part = tokens // BLOCK
    smem, vmem = pl.BlockSpec(memory_space=pltpu.SMEM), pl.BlockSpec(memory_space=pltpu.VMEM)
    given = [d for d in dq_in if d is not None]
    args = [ranks, nvis, diag, *packed, *kvs, *given, *(dkv_in or [])]
    dq_shapes = [
        jax.ShapeDtypeStruct((per_part, head_dim, cols), F32) if d is None else jax.ShapeDtypeStruct((tokens, width), d)
        for d in dq_out
    ]
    dkv_shapes = [jax.ShapeDtypeStruct(kv.shape, d) for kv, d in zip(kvs, dkv_dtypes)]
    flops = 10 * count * cols * rows * head_dim // 2
    out = pl.pallas_call(
        functools.partial(
            grads_kernel,
            parts=parts,
            pieces=pieces,
            dq_in=tuple(int(d is not None) for d in dq_in),
            dkv_in=bool(dkv_in),
            dq_final=tuple(d is not None for d in dq_out),
            dkv_final=dkv_final,
            heads=heads,
            head_dim=head_dim,
        ),
        out_shape=tuple(dq_shapes + dkv_shapes),
        in_specs=[smem] * 3 + [vmem] * (len(args) - 3),
        out_specs=(vmem,) * (parts + pieces),
        scratch_shapes=[
            pltpu.VMEM((rows, head_dim), BF16),
            pltpu.VMEM((rows, head_dim), BF16),
            pltpu.VMEM((cols, head_dim), BF16),
            pltpu.VMEM((cols, head_dim), BF16),
            pltpu.VMEM((head_dim, cols), BF16),
            pltpu.VMEM((head_dim, cols), BF16),
            pltpu.VMEM((head_dim, cols), F32),
            pltpu.VMEM((rows, head_dim), F32),
            pltpu.VMEM((rows, head_dim), F32),
            pltpu.VMEM((2, count, cols), F32),
        ],
        compiler_params=pltpu.CompilerParams(vmem_limit_bytes=28 * 2**20),
        cost_estimate=pl.CostEstimate(flops=flops, bytes_accessed=2**23, transcendentals=count * cols * rows // 2),
    )(*args)
    return out[:parts], out[parts:]


def body(query, key, value, output, grad_out, lse, block_order):
    tokens_here = query.shape[0]
    per_device = tokens_here // BLOCK
    head_count = lse.shape[0]
    head_dim = key.shape[1]
    inner_count = lax.axis_size("inner")
    outer_count = lax.axis_size("outer")
    inner_index = lax.axis_index("inner")
    outer_index = lax.axis_index("outer")

    def moved(x, by, second):
        pairs = []
        for i in range(inner_count):
            y, x_at = divmod(i, SIDE)
            for o in range(outer_count):
                if (o % 2 == 0) != second:
                    to = y * SIDE + (x_at + by) % SIDE
                else:
                    to = (y + by) % SIDE * SIDE + x_at
                pairs.append((i * outer_count + o, to * outer_count + o))
        return lax.ppermute(x, ("inner", "outer"), pairs)

    def to_group(x, by):
        return lax.ppermute(x, "outer", [(i, (i + by) % outer_count) for i in range(outer_count)])

    zero = jnp.zeros((), BF16)
    kv = lax.pad(key, zero, ((0, 0, 0), (0, head_dim, 0))) + lax.pad(value, zero, ((0, 0, 0), (head_dim, 0, 0)))
    row = [kv] + [moved(kv, by, False) for by in STEPS[1:]]
    mine = pack(query, grad_out, output, lse)
    following = to_group(mine, -1)
    own_row = jnp.concatenate(row, axis=0)
    own_row, block_order = lax.optimization_barrier((own_row, block_order))
    rows = [own_row] + [moved(own_row, by, True) for by in STEPS[1:]]

    ids = block_order.reshape(inner_count, outer_count, per_device)
    first = jnp.array(STEPS, jnp.int32)[None, :]
    second = jnp.array(STEPS, jnp.int32)[:, None]
    y, x = inner_index // SIDE, inner_index % SIDE
    even = outer_index % 2 == 0
    from_y = (y - jnp.where(even, second, first)) % SIDE
    from_x = (x - jnp.where(even, first, second)) % SIDE
    owner = (from_y * SIDE + from_x).reshape(-1)
    group_ids = lax.dynamic_index_in_dim(ids, outer_index, 1, keepdims=False)
    key_ids = jnp.take(group_ids, owner, axis=0).reshape(-1)
    own_ids = lax.dynamic_index_in_dim(group_ids, inner_index, 0, keepdims=False)
    next_ids = lax.dynamic_index_in_dim(
        lax.dynamic_index_in_dim(ids, (outer_index + 1) % outer_count, 1, keepdims=False),
        inner_index,
        0,
        keepdims=False,
    )
    query_ids = jnp.concatenate([own_ids, next_ids])

    def order(keys):
        return jnp.sum((keys[None, :] < keys[:, None]).astype(jnp.int32), axis=1)

    def seen(keys, queries):
        return (
            jnp.sum((keys[None, :] <= queries[:, None]).astype(jnp.int32), axis=1),
            jnp.sum((keys[None, :] == queries[:, None]).astype(jnp.int32), axis=1),
        )

    row_ids, other_ids = jnp.split(key_ids, [own_row.shape[0] // BLOCK])
    row_rank = order(row_ids)
    (dq_own,), (dkv_row,) = grads(
        row_rank, *seen(row_ids, own_ids), [mine], [own_row],
        [None], None, [None], [F32], False,
    )
    (dq_own, dq_next), dkv_rows = grads(
        order(other_ids), *seen(other_ids, query_ids), [mine, following], rows[1:],
        [dq_own, None], None, [F32, None], [BF16] * 3, True,
    )
    (dq_next,), (row_sum,) = grads(
        row_rank, *seen(row_ids, next_ids), [following], [own_row],
        [dq_next], [dkv_row], [BF16], [F32], True,
    )
    dq_back = to_group(dq_next, 1)
    for by, part in zip(STEPS[1:], dkv_rows):
        row_sum = row_sum + moved(part, -by, True).astype(F32)
    row_low = row_sum.astype(BF16)
    total = row_sum[:tokens_here]
    for at, by in enumerate(STEPS[1:], 1):
        total = total + moved(row_low[at * tokens_here : (at + 1) * tokens_here], -by, False).astype(F32)
    return (
        (dq_own + dq_back.astype(F32)).astype(BF16),
        total[:, :head_dim].astype(BF16),
        total[:, head_dim:].astype(BF16),
    )


def solution(mesh):
    tokens = P(("inner", "outer"), "head")
    return jax.shard_map(
        body,
        mesh=mesh,
        in_specs=(tokens, tokens, tokens, tokens, tokens, P("head", ("inner", "outer")), P("head")),
        out_specs=(tokens, tokens, tokens),
        check_vma=False,
    )
```

```python
import functools
import math

import jax
import jax.numpy as jnp
from jax import lax
from jax.experimental import pallas as pl
from jax.experimental.pallas import tpu as pltpu
from jax.sharding import PartitionSpec as P

BLOCK = 64
SIDE = 4
UNIT = 256
GROUP = 4
BF16 = jnp.bfloat16
F32 = jnp.float32
STEPS = (0, 1, -1, 2)
PIECES = ((0, 0), (0, 1), (1, 0))


def dot(a, b):
    return jnp.dot(a, b, preferred_element_type=F32)


def grads_kernel(*refs, parts, pieces, dq_in, dkv_in, dq_final, dkv_final, finish, tokens, heads, head_dim):
    refs = list(refs)

    def take(n):
        out, refs[:] = refs[:n], refs[n:]
        return out

    rank_ref, nvis_ref, diag_ref = take(3)
    packed_refs = take(parts)
    kv_refs = take(pieces)
    dq_in_refs = take(sum(dq_in))
    dkv_in_refs = take(pieces if dkv_in else 0)
    finish_refs = take(finish)
    dq_refs = take(parts)
    dkv_refs = take(pieces)
    done_refs = take(finish)
    ks, vs, qs, dos, qt, dot_t, dqt, dka, dva, stat = take(10)

    scaling = head_dim**-0.5
    rate = scaling * math.log2(math.e)
    cols = heads * BLOCK
    per_part = tokens // BLOCK
    per_piece = kv_refs[0].shape[0] // BLOCK

    for at, kv_ref in enumerate(kv_refs):

        @pl.loop(0, per_piece, unroll=4)
        def _(j, at=at, kv_ref=kv_ref):
            src = pl.multiple_of(j * BLOCK, BLOCK)
            dst = pl.multiple_of(rank_ref[at * per_piece + j] * BLOCK, BLOCK)
            ks[pl.ds(dst, BLOCK), :] = kv_ref[pl.ds(src, BLOCK), :head_dim]
            vs[pl.ds(dst, BLOCK), :] = kv_ref[pl.ds(src, BLOCK), head_dim:]
            if dkv_in:
                dka[pl.ds(dst, BLOCK), :] = dkv_in_refs[at][pl.ds(src, BLOCK), :head_dim]
                dva[pl.ds(dst, BLOCK), :] = dkv_in_refs[at][pl.ds(src, BLOCK), head_dim:]

    if not dkv_in:
        dka[...] = jnp.zeros_like(dka)
        dva[...] = jnp.zeros_like(dva)

    span = 2 * per_part
    for part, packed in enumerate(packed_refs):
        tail = packed[2 * tokens :, :].astype(F32)
        pieces_of = [
            tail[down * span : (down + 1) * span, lanes * cols : (lanes + 1) * cols] for down, lanes in PIECES
        ]
        stat[part * span : (part + 1) * span, :] = pieces_of[0] + pieces_of[1] + pieces_of[2]

    token = lax.broadcasted_iota(jnp.int32, (1, cols), 1) % BLOCK

    for part in range(parts):
        first = part * per_part
        given = dq_in_refs[sum(dq_in[:part])] if dq_in[part] else None

        @pl.loop(0, per_part)
        def _(i, part=part, first=first, given=given):
            n = first + i
            rows_here = pl.ds(pl.multiple_of(i * BLOCK, BLOCK), BLOCK)
            grad_rows_here = pl.ds(pl.multiple_of(tokens + i * BLOCK, BLOCK), BLOCK)
            for h in range(heads):
                lanes = slice(h * head_dim, (h + 1) * head_dim)
                qs[h * BLOCK : (h + 1) * BLOCK, :] = packed_refs[part][rows_here, lanes]
                dos[h * BLOCK : (h + 1) * BLOCK, :] = packed_refs[part][grad_rows_here, lanes]
            qt[...] = qs[...].T
            dot_t[...] = dos[...].T
            dqt[...] = jnp.zeros((head_dim, cols), F32) if given is None else given[i]
            visible = nvis_ref[n]
            units = (visible + (UNIT // BLOCK - 1)) // (UNIT // BLOCK)
            lse_row = stat[pl.ds(part * span + i, 1), :] * math.log2(math.e)
            delta_row = stat[pl.ds(part * span + per_part + i, 1), :]
            limit = jnp.where(diag_ref[n] > 0, token, BLOCK - 1) + (visible - 1) * BLOCK

            def tile(unit, number, masked):
                for u in range(number):
                    start = pl.multiple_of((unit + u) * UNIT, UNIT)
                    here = pl.ds(start, UNIT)
                    scores = dot(ks[here, :], qt[...])
                    grad_probs = dot(vs[here, :], dot_t[...])
                    probs = jnp.exp2(scores * rate - lse_row)
                    if masked:
                        row = lax.broadcasted_iota(jnp.int32, (UNIT, cols), 0)
                        probs = jnp.where(row <= limit - start, probs, 0.0)
                    grad_scores = (probs * (grad_probs - delta_row)).astype(BF16)
                    dva[here, :] += dot(probs.astype(BF16), dos[...])
                    dka[here, :] += dot(grad_scores, qs[...])
                    dqt[...] += lax.dot_general(
                        ks[here, :], grad_scores, (((0,), (0,)), ((), ())), preferred_element_type=F32
                    )

            clear = jnp.maximum(units - 1, 0) // GROUP
            rest = units - clear * GROUP

            @pl.loop(0, clear)
            def _(t):
                tile(t * GROUP, GROUP, False)

            for count in range(1, GROUP + 1):

                @pl.when(rest == count)
                def _(count=count):
                    tile(clear * GROUP, count, True)

            if dq_final[part]:
                rows_out = (dqt[...] * scaling).astype(dq_refs[part].dtype).T
                for h in range(heads):
                    dq_refs[part][rows_here, h * head_dim : (h + 1) * head_dim] = rows_out[
                        h * BLOCK : (h + 1) * BLOCK, :
                    ]
            else:
                dq_refs[part][i] = dqt[...]

    for sums, done in zip(finish_refs, done_refs):

        @pl.loop(0, per_part)
        def _(i, sums=sums, done=done):
            rows_here = pl.ds(pl.multiple_of(i * BLOCK, BLOCK), BLOCK)
            rows_out = (sums[i] * scaling).T
            for h in range(heads):
                done[rows_here, h * head_dim : (h + 1) * head_dim] = rows_out[h * BLOCK : (h + 1) * BLOCK, :]

    for at, dkv_ref in enumerate(dkv_refs):

        @pl.loop(0, per_piece, unroll=4)
        def _(j, at=at, dkv_ref=dkv_ref):
            dst = pl.multiple_of(j * BLOCK, BLOCK)
            src = pl.multiple_of(rank_ref[at * per_piece + j] * BLOCK, BLOCK)
            factor = scaling if dkv_final else 1.0
            dkv_ref[pl.ds(dst, BLOCK), :head_dim] = (dka[pl.ds(src, BLOCK), :] * factor).astype(dkv_ref.dtype)
            dkv_ref[pl.ds(dst, BLOCK), head_dim:] = dva[pl.ds(src, BLOCK), :].astype(dkv_ref.dtype)


def pack_kernel(q_ref, do_ref, out_ref, lse_ref, packed_ref, out_here, stat, tail, sems, *, heads, head_dim):
    rows = q_ref.shape[0]
    copies = [
        pltpu.make_async_copy(do_ref, packed_ref.at[rows : 2 * rows, :], sems.at[0]),
        pltpu.make_async_copy(out_ref, out_here, sems.at[1]),
        pltpu.make_async_copy(lse_ref, stat.at[:heads, :], sems.at[2]),
        pltpu.make_async_copy(q_ref, packed_ref.at[:rows, :], sems.at[3]),
    ]
    for copy in copies:
        copy.start()
    for copy in copies[:3]:
        copy.wait()
    for h in range(heads):
        lanes = slice(h * head_dim, (h + 1) * head_dim)
        product = packed_ref[rows : 2 * rows, lanes].astype(F32) * out_here[:, lanes].astype(F32)
        stat[heads + h : heads + h + 1, :] = jnp.sum(product.T, axis=0, keepdims=True)
    blocks, cols = rows // BLOCK, heads * BLOCK
    count = 2 * blocks
    tail[...] = jnp.zeros_like(tail)
    for kind in range(2):
        for i in range(blocks):
            for h in range(heads):
                tail[kind * blocks + i : kind * blocks + i + 1, h * BLOCK : (h + 1) * BLOCK] = stat[
                    kind * heads + h : kind * heads + h + 1, i * BLOCK : (i + 1) * BLOCK
                ]
    left = tail[:count, :cols]
    for down, lanes in PIECES:
        low = left.astype(BF16).astype(F32)
        tail[down * count : (down + 1) * count, lanes * cols : (lanes + 1) * cols] = low
        left = left - low
    packed_ref[2 * rows :, :] = tail[...].astype(BF16)
    copies[3].wait()


def pack(query, grad_out, output, lse):
    heads, rows = lse.shape
    tail = 4 * (rows // BLOCK)
    return pl.pallas_call(
        functools.partial(pack_kernel, heads=heads, head_dim=query.shape[1] // heads),
        out_shape=jax.ShapeDtypeStruct((2 * rows + tail, query.shape[1]), BF16),
        in_specs=[pl.BlockSpec(memory_space=pltpu.HBM)] * 4,
        out_specs=pl.BlockSpec(memory_space=pltpu.VMEM),
        scratch_shapes=[
            pltpu.VMEM((rows, query.shape[1]), BF16),
            pltpu.VMEM((2 * heads, rows), F32),
            pltpu.VMEM((tail, query.shape[1]), F32),
            pltpu.SemaphoreType.DMA((4,)),
        ],
        compiler_params=pltpu.CompilerParams(vmem_limit_bytes=60 * 2**20),
        cost_estimate=pl.CostEstimate(flops=2 * query.size, bytes_accessed=2**22, transcendentals=0),
    )(query, grad_out, output, lse)


def grads(ranks, nvis, diag, packed, kvs, dq_in, dkv_in, dq_out, dkv_dtypes, dkv_final, dq_tokens, finish=()):
    parts, pieces = len(packed), len(kvs)
    head_dim = kvs[0].shape[1] // 2
    width = packed[0].shape[1]
    heads = width // head_dim
    cols = heads * BLOCK
    count = nvis.shape[0]
    rows = sum(kv.shape[0] for kv in kvs)
    tokens = dq_tokens
    per_part = tokens // BLOCK
    smem, vmem = pl.BlockSpec(memory_space=pltpu.SMEM), pl.BlockSpec(memory_space=pltpu.VMEM)
    given = [d for d in dq_in if d is not None]
    args = [ranks, nvis, diag, *packed, *kvs, *given, *(dkv_in or []), *finish]
    dq_shapes = [
        jax.ShapeDtypeStruct((per_part, head_dim, cols), F32) if d is None else jax.ShapeDtypeStruct((tokens, width), d)
        for d in dq_out
    ]
    dkv_shapes = [jax.ShapeDtypeStruct(kv.shape, d) for kv, d in zip(kvs, dkv_dtypes)]
    done_shapes = [jax.ShapeDtypeStruct((tokens, width), F32)] * len(finish)
    flops = 10 * count * cols * rows * head_dim // 2
    out = pl.pallas_call(
        functools.partial(
            grads_kernel,
            parts=parts,
            pieces=pieces,
            dq_in=tuple(int(d is not None) for d in dq_in),
            dkv_in=bool(dkv_in),
            dq_final=tuple(d is not None for d in dq_out),
            dkv_final=dkv_final,
            tokens=tokens,
            finish=len(finish),
            heads=heads,
            head_dim=head_dim,
        ),
        out_shape=tuple(dq_shapes + dkv_shapes + done_shapes),
        in_specs=[smem] * 3 + [vmem] * (len(args) - 3),
        out_specs=(vmem,) * (parts + pieces + len(finish)),
        scratch_shapes=[
            pltpu.VMEM((rows, head_dim), BF16),
            pltpu.VMEM((rows, head_dim), BF16),
            pltpu.VMEM((cols, head_dim), BF16),
            pltpu.VMEM((cols, head_dim), BF16),
            pltpu.VMEM((head_dim, cols), BF16),
            pltpu.VMEM((head_dim, cols), BF16),
            pltpu.VMEM((head_dim, cols), F32),
            pltpu.VMEM((rows, head_dim), F32),
            pltpu.VMEM((rows, head_dim), F32),
            pltpu.VMEM((2 * count, cols), F32),
        ],
        compiler_params=pltpu.CompilerParams(vmem_limit_bytes=28 * 2**20),
        cost_estimate=pl.CostEstimate(flops=flops, bytes_accessed=2**23, transcendentals=count * cols * rows // 2),
    )(*args)
    return out[:parts], out[parts : parts + pieces], out[parts + pieces :]


def body(query, key, value, output, grad_out, lse, block_order):
    tokens_here = query.shape[0]
    per_device = tokens_here // BLOCK
    head_count = lse.shape[0]
    head_dim = key.shape[1]
    inner_count = lax.axis_size("inner")
    outer_count = lax.axis_size("outer")
    inner_index = lax.axis_index("inner")
    outer_index = lax.axis_index("outer")

    def moved(x, by, second):
        pairs = []
        for i in range(inner_count):
            y, x_at = divmod(i, SIDE)
            for o in range(outer_count):
                if (o % 2 == 0) != second:
                    to = y * SIDE + (x_at + by) % SIDE
                else:
                    to = (y + by) % SIDE * SIDE + x_at
                pairs.append((i * outer_count + o, to * outer_count + o))
        return lax.ppermute(x, ("inner", "outer"), pairs)

    def to_group(x, by):
        return lax.ppermute(x, "outer", [(i, (i + by) % outer_count) for i in range(outer_count)])

    zero = jnp.zeros((), BF16)
    kv = lax.pad(key, zero, ((0, 0, 0), (0, head_dim, 0))) + lax.pad(value, zero, ((0, 0, 0), (head_dim, 0, 0)))
    row = [kv] + [moved(kv, by, False) for by in STEPS[1:]]
    mine = pack(query, grad_out, output, lse)
    following = to_group(mine, -1)
    own_row = jnp.concatenate(row, axis=0)
    own_row, block_order = lax.optimization_barrier((own_row, block_order))
    rows = [own_row] + [moved(own_row, by, True) for by in STEPS[1:]]

    ids = block_order.reshape(inner_count, outer_count, per_device)
    first = jnp.array(STEPS, jnp.int32)[None, :]
    second = jnp.array(STEPS, jnp.int32)[:, None]
    y, x = inner_index // SIDE, inner_index % SIDE
    even = outer_index % 2 == 0
    from_y = (y - jnp.where(even, second, first)) % SIDE
    from_x = (x - jnp.where(even, first, second)) % SIDE
    owner = (from_y * SIDE + from_x).reshape(-1)
    group_ids = lax.dynamic_index_in_dim(ids, outer_index, 1, keepdims=False)
    key_ids = jnp.take(group_ids, owner, axis=0).reshape(-1)
    own_ids = lax.dynamic_index_in_dim(group_ids, inner_index, 0, keepdims=False)
    next_ids = lax.dynamic_index_in_dim(
        lax.dynamic_index_in_dim(ids, (outer_index + 1) % outer_count, 1, keepdims=False),
        inner_index,
        0,
        keepdims=False,
    )
    query_ids = jnp.concatenate([own_ids, next_ids])

    def order(keys):
        return jnp.sum((keys[None, :] < keys[:, None]).astype(jnp.int32), axis=1)

    def seen(keys, queries):
        return (
            jnp.sum((keys[None, :] <= queries[:, None]).astype(jnp.int32), axis=1),
            jnp.sum((keys[None, :] == queries[:, None]).astype(jnp.int32), axis=1),
        )

    row_ids, other_ids = jnp.split(key_ids, [own_row.shape[0] // BLOCK])
    row_rank = order(row_ids)
    (dq_own,), (dkv_row,), _ = grads(
        row_rank, *seen(row_ids, own_ids), [mine], [own_row], [None], None, [None], [F32], False, tokens_here
    )
    (dq_own, dq_next), dkv_rows, _ = grads(
        order(other_ids), *seen(other_ids, query_ids), [mine, following], rows[1:],
        [dq_own, None], None, [None, None], [BF16] * 3, True, tokens_here,
    )
    (dq_next,), (row_sum,), (dq_own,) = grads(
        row_rank, *seen(row_ids, next_ids), [following], [own_row],
        [dq_next], [dkv_row], [BF16], [F32], True, tokens_here, [dq_own],
    )
    dq_back = to_group(dq_next, 1)
    for by, part in zip(STEPS[1:], dkv_rows):
        row_sum = row_sum + moved(part, -by, True).astype(F32)
    row_low = row_sum.astype(BF16)
    total = row_sum[:tokens_here]
    for at, by in enumerate(STEPS[1:], 1):
        total = total + moved(row_low[at * tokens_here : (at + 1) * tokens_here], -by, False).astype(F32)
    return (
        (dq_own + dq_back.astype(F32)).astype(BF16),
        total[:, :head_dim].astype(BF16),
        total[:, head_dim:].astype(BF16),
    )


def solution(mesh):
    tokens = P(("inner", "outer"), "head")
    return jax.shard_map(
        body,
        mesh=mesh,
        in_specs=(tokens, tokens, tokens, tokens, tokens, P("head", ("inner", "outer")), P("head")),
        out_specs=(tokens, tokens, tokens),
        check_vma=False,
    )
```
